128 devices in a mesh: replica: 16 (over x, z_lo, core), tensor: 8 (over z_hi, y).
Axes of the slice: x: 4, y: 4, z: 4 (z_hi: 2, z_lo: 2; z = z_hi * 2 + z_lo), core: 2. Of those that a mesh axis runs over, the one named last changes fastest.
Arguments:
- prompt: bfloat16 [16384, 6144], P('replica', 'tensor'), may hold values from -6 to 6
- dec_tokens: bfloat16 [64, 6144], P('replica', 'tensor'), may hold values from -6 to 6
- w_query: bfloat16 [6144, 6144], P(None, 'tensor'), may hold values from -0.078125 to 0.078125
- w_keyval: bfloat16 [6144, 2048], P(None, 'tensor'), may hold values from -0.078125 to 0.078125
- prefix_cache: bfloat16 [32, 1024, 2048], P('replica', None, 'tensor'), may hold values from -6 to 6
- prompt_len: int32 [32], replicated, may hold values from 256 to 512, as said below
- fill_len: int32 [32], replicated, may hold values from 256 to 1024, as said below
- owner: int32 [32], replicated, may hold values from 0 to 31, each once
Outputs:
- prefill_out: bfloat16 [16384, 6144], P('replica', 'tensor')
- decode_out: bfloat16 [64, 6144], P('replica', 'tensor')
- decode_cache: bfloat16 [32, 1536, 2048], P('replica', None, 'tensor')
The draws below stay inside these ranges and needn't reach their ends.
Inputs may be any that keep to these rules, and one draw needn't show every extreme that they name: Each request's new prompt fills the first prompt_len slots of its 512; some request has 512 and some 512 // 2. `fill_len`: some request has 1024 and some 1024 // 4. `owner`: a permutation; decode row s lies on replica s // 2.
All inputs are finite; a program needn't handle non-finite values.
Results may differ from the reference program's by a relative error of at most 0.0095.
Values may be sent and summed in bfloat16 or wider, within the bound.
No kernel may reach another device: no remote copies, remote signals or barrier semaphores. Data moves between devices by JAX's collectives and lax.ppermute only.
A program may use at most 128 MiB of HBM per device.

```python
import math
import jax
import jax.numpy as jnp
from jax import lax

D = 6144
HEADS = 48
KV = 8
HD = 128
PROMPT = 512
CTX = 1024
REQ = 32


def draw_prompt_len(key, part):
    key = jax.random.fold_in(key, 11)
    first_key, second_key = jax.random.split(key)
    counts = jax.random.randint(first_key, (REQ,), PROMPT // 2, PROMPT + 1).astype(jnp.int32)
    order = jax.random.permutation(second_key, REQ)
    counts = counts.at[order[0]].set(PROMPT)
    return counts.at[order[1]].set(PROMPT // 2)


def draw_fill_len(key, part):
    key = jax.random.fold_in(key, 23)
    first_key, second_key = jax.random.split(key)
    counts = jax.random.randint(first_key, (REQ,), CTX // 4, CTX + 1).astype(jnp.int32)
    order = jax.random.permutation(second_key, REQ)
    counts = counts.at[order[0]].set(CTX)
    return counts.at[order[1]].set(CTX // 4)


def steps_of(key, shape, cuts, smallest, high):
    level = 1.0
    for position, blocks in cuts:
        draws = jax.random.uniform(jax.random.fold_in(jax.random.fold_in(key, 6), position), (blocks,), jnp.float32, smallest / len(cuts), high / len(cuts))
        level = level * jnp.repeat(jnp.exp(draws), shape[position] // blocks).reshape((-1,) + (1,) * (len(shape) - 1 - position))
    return level


def noise(key, shape, deviation, reach, shards=(), held_as=jnp.bfloat16):
    array = deviation * jax.random.normal(key, shape, jnp.float32)
    if shards:
        array = array * steps_of(key, shape, shards, -0.22, 0.18)
    return jnp.clip(array, -reach, reach).astype(held_as)


def setup_inputs(seed: int = 0) -> dict:
    keys = jax.random.split(jax.random.key(seed), 9)
    return {
        "prompt": noise(keys[0], (REQ * PROMPT, D), 1.0, 6.0, ((0, 16), (1, 8))),
        "dec_tokens": noise(keys[1], (REQ * 2, D), 1.0, 6.0, ((0, 16), (1, 8))),
        "w_query": noise(keys[2], (D, HEADS * HD), D ** -0.5, 0.078125, ((1, 8),)),
        "w_keyval": noise(keys[3], (D, KV * 2 * HD), D ** -0.5, 0.078125, ((1, 8),)),
        "prefix_cache": noise(keys[4], (REQ, CTX, KV * 2 * HD), 1.0, 6.0, ((0, 16), (2, 8))),
        "prompt_len": draw_prompt_len(jax.random.fold_in(keys[8], 71), 0),
        "fill_len": draw_fill_len(jax.random.fold_in(keys[8], 71), 0),
        "owner": jax.random.permutation(keys[7], REQ).astype(jnp.int32),
    }


LOW_SCORE = -1e+30
FULL_PREC = lax.Precision.HIGHEST

def prompt_head(query_rows, key_rows, values, fill_count, live_len):
    ctx_len = key_rows.shape[0] - query_rows.shape[0]
    score_scale = 1.0 / math.sqrt(query_rows.shape[1])
    scores = jnp.dot(query_rows, key_rows.T, preferred_element_type=jnp.float32) * score_scale
    key_pos = jnp.arange(key_rows.shape[0], dtype=jnp.int32)[None, :]
    query_pos = ctx_len + jnp.arange(query_rows.shape[0], dtype=jnp.int32)[:, None]
    inside = (key_pos < fill_count) | (key_pos >= ctx_len) & (key_pos <= query_pos) & (key_pos < ctx_len + live_len)
    masked = jnp.where(inside, scores, LOW_SCORE)
    row_top = lax.optimization_barrier(jnp.max(masked, axis=1, keepdims=True))
    weights = jnp.where(inside, jnp.exp(masked - row_top), 0.0)
    row_total = lax.optimization_barrier(jnp.sum(weights, axis=1, keepdims=True))
    attended = jnp.dot(weights.astype(jnp.bfloat16), values, preferred_element_type=jnp.float32) / row_total
    return jnp.where(query_pos < ctx_len + live_len, attended, 0.0).astype(jnp.bfloat16)

def prefill_heads(query_stack, cache_stack, fills, lengths):

    def per_pair(member):
        query_group, keyval, fill_count, live_len = member
        return lax.map(lambda query_rows: prompt_head(query_rows, keyval[0], keyval[1], fill_count, live_len), query_group)
    return lax.map(per_pair, (query_stack, cache_stack, fills, lengths))

def reference(prompt, dec_tokens, w_query, w_keyval, prefix_cache, prompt_len, fill_len, owner):
    request_count = prefix_cache.shape[0]
    ctx_len = prefix_cache.shape[1]
    new_len = prompt.shape[0] // request_count
    dec_steps = dec_tokens.shape[0] // request_count
    group_size = HEADS // KV
    total_len = ctx_len + new_len
    queries = jnp.dot(prompt, w_query, preferred_element_type=jnp.float32).astype(jnp.bfloat16)
    keyvals = jnp.dot(prompt, w_keyval, preferred_element_type=jnp.float32).astype(jnp.bfloat16)
    full = jnp.concatenate([prefix_cache.reshape(request_count, ctx_len, KV, 2, HD), keyvals.reshape(request_count, new_len, KV, 2, HD)], axis=1)
    query_stack = queries.reshape(request_count, new_len, KV, group_size, HD).transpose(0, 2, 3, 1, 4).reshape(request_count * KV, group_size, new_len, HD)
    cache_stack = full.transpose(0, 2, 3, 1, 4).reshape(request_count * KV, 2, total_len, HD)
    attended = prefill_heads(query_stack, cache_stack, jnp.repeat(fill_len, KV), jnp.repeat(prompt_len, KV))
    prefill_out = attended.reshape(request_count, KV, group_size, new_len, HD).transpose(0, 3, 1, 2, 4).reshape(request_count * new_len, HEADS * HD)
    dec_query = jnp.dot(dec_tokens, w_query, preferred_element_type=jnp.float32).astype(jnp.bfloat16).reshape(request_count, dec_steps, KV, group_size, HD)
    dec_keyval = jnp.dot(dec_tokens, w_keyval, preferred_element_type=jnp.float32).astype(jnp.bfloat16).reshape(request_count, dec_steps, KV, 2, HD)
    slot_ids = jnp.arange(request_count, dtype=jnp.int32)
    source = lax.optimization_barrier(jnp.sum(jnp.where(owner[None, :] == slot_ids[:, None], slot_ids[None, :], 0), axis=1)).astype(jnp.int32)
    positions = jnp.arange(total_len, dtype=jnp.int32)
    live_all = (positions[None, :] < fill_len[:, None]) | (positions[None, :] >= ctx_len) & (positions[None, :] < ctx_len + prompt_len[:, None])
    zeroed = jnp.where(live_all[:, :, None, None, None], full, jnp.zeros((), full.dtype)).astype(full.dtype)
    decode_cache = jnp.take(zeroed, source, axis=0).reshape(request_count, total_len, KV * 2 * HD)
    causal = (jnp.arange(dec_steps)[None, :] <= jnp.arange(dec_steps)[:, None])[:, None, None, :]
    score_scale = 1.0 / math.sqrt(HD)

    def decode_slot(member):
        slot_query, slot_keyval, request = member
        cache = lax.dynamic_index_in_dim(full, request, 0, keepdims=False)
        fill_count = lax.dynamic_index_in_dim(fill_len, request, 0, keepdims=False)
        live_len = lax.dynamic_index_in_dim(prompt_len, request, 0, keepdims=False)
        inside = (positions < fill_count) | (positions >= ctx_len) & (positions < ctx_len + live_len)
        query_rows = slot_query.astype(jnp.float32)
        older = jnp.einsum('tkgd,skd->tkgs', query_rows, cache[:, :, 0].astype(jnp.float32), precision=FULL_PREC) * score_scale
        newer = jnp.einsum('tkgd,ukd->tkgu', query_rows, slot_keyval[:, :, 0].astype(jnp.float32), precision=FULL_PREC) * score_scale
        older = jnp.where(inside, older, LOW_SCORE)
        newer = jnp.where(causal, newer, LOW_SCORE)
        row_top = jnp.maximum(lax.optimization_barrier(jnp.max(older, axis=3)), lax.optimization_barrier(jnp.max(newer, axis=3)))[..., None]
        older_w = jnp.where(inside, jnp.exp(older - row_top), 0.0)
        newer_w = jnp.where(causal, jnp.exp(newer - row_top), 0.0)
        row_total = lax.optimization_barrier(jnp.sum(older_w, axis=3)) + lax.optimization_barrier(jnp.sum(newer_w, axis=3))
        attended_rows = jnp.einsum('tkgs,skd->tkgd', older_w, cache[:, :, 1].astype(jnp.float32), precision=FULL_PREC)
        attended_rows = attended_rows + jnp.einsum('tkgu,ukd->tkgd', newer_w, slot_keyval[:, :, 1].astype(jnp.float32), precision=FULL_PREC)
        return (attended_rows / row_total[..., None]).astype(jnp.bfloat16)
    decode_out = lax.map(decode_slot, (dec_query, dec_keyval, source)).reshape(request_count * dec_steps, HEADS * HD)
    return (prefill_out, decode_out, decode_cache)
```

```python
import functools
import math

import jax
import jax.numpy as jnp
from jax import lax
from jax.experimental import pallas as pl
from jax.experimental.pallas import tpu as pltpu
from jax.sharding import PartitionSpec as P

HEADS = 48
KV = 8
HD = 128
GROUP = HEADS // KV
STEPS = 2
DEC_ROWS = 16
KEY_BLOCK = 256
MIB = 1024 * 1024

LOW_SCORE = -1e30
EXP_SCALE = math.log2(math.e) / math.sqrt(HD)


def dot_nt(a, b):
    return lax.dot_general(a, b, (((1,), (1,)), ((), ())), preferred_element_type=jnp.float32)


def dot_nn(a, b):
    return lax.dot_general(a, b, (((1,), (0,)), ((), ())), preferred_element_type=jnp.float32)


def row_tiles(counts):
    tiles = []
    start = 0
    for count in counts:
        first = (count // 2 + 15) // 16 * 16
        tiles += [(start, first), (start + first, count - first)]
        start += count
    return tiles


def project_kernel(shape, has_start, widths, ids, *refs):
    groups, counts, depth = shape
    refs = list(refs)
    pieces = [[refs.pop(0) for _ in counts] for _ in range(groups)]
    weights = [refs.pop(0) for _ in widths]
    start_ref = refs.pop(0) if has_start else None
    held, weight_held, total, sems = refs[-4:]
    outs = refs[:-4]
    offsets = [sum(counts[:i]) for i in range(len(counts))]
    columns = [sum(widths[:i]) for i in range(len(widths))]
    per = 1

    def copies(k):
        made = []
        for j in range(k * per, (k + 1) * per):
            at = pl.ds((j - k * per) * depth, depth)
            for i, count in enumerate(counts):
                made.append((pieces[j][i], held.at[k, pl.ds(offsets[i], count), at]))
            half = depth // 2
            for i, width in enumerate(widths):
                for part in range(2):
                    src = pl.ds(pl.multiple_of(ids[j] * depth + part * half, half), half)
                    dst = pl.ds((j - k * per) * depth + part * half, half)
                    made.append(
                        (
                            weights[i].at[src, :],
                            weight_held.at[k, dst, pl.ds(columns[i], width)],
                        )
                    )
        return [
            pltpu.make_async_copy(src, dst, sems.at[k, n]) for n, (src, dst) in enumerate(made)
        ]

    steps = groups // per
    for k in range(steps):
        for copy in copies(k):
            copy.start()
    all_columns = sum(widths)
    for k in range(steps):
        for copy in copies(k):
            copy.wait()
        for row, count in row_tiles(counts):
            for col in range(0, all_columns, 512):
                width = min(512, all_columns - col)
                at = (slice(row, row + count), slice(col, col + width))
                part = dot_nn(held[k, row : row + count, :], weight_held[k, :, col : col + width])
                if k:
                    part = part + total[at]
                elif has_start:
                    part = part + start_ref[row : row + count, col : col + width]
                if k < steps - 1:
                    total[at] = part
                    continue
                if outs[0].dtype == jnp.float32:
                    group = max(i for i, offset in enumerate(offsets) if offset <= row)
                    low = row - offsets[group]
                    outs[group][low : low + count, col : col + width] = part
                    continue
                for out, first, wide in zip(outs, columns, widths):
                    low, high = max(first, col), min(first + wide, col + width)
                    if low < high:
                        value = part[:, low - col : high - col].astype(jnp.bfloat16)
                        out[row : row + count, low - first : high - first] = value


def project(pieces, ids, weights, start=None, start_col=0, out_type=jnp.bfloat16):
    groups = len(pieces)
    counts = tuple(x.shape[0] for x in pieces[0])
    depth = pieces[0][0].shape[1]
    widths = tuple(w.shape[1] for w in weights)
    rows, columns = sum(counts), sum(widths)
    has_start = start is not None
    operands = [x for group in pieces for x in group] + list(weights)
    in_specs = [pl.BlockSpec(memory_space=pltpu.HBM)] * len(operands)
    if has_start:
        in_specs.append(pl.BlockSpec((rows, columns), lambda *_: (0, start_col // columns)))
        operands.append(start)
    if out_type == jnp.float32:
        out_shape = [jax.ShapeDtypeStruct((count, columns), jnp.float32) for count in counts]
    else:
        out_shape = [jax.ShapeDtypeStruct((rows, w), jnp.bfloat16) for w in widths]
    per = 1
    copies = per * (len(counts) + 2 * len(widths))
    return pl.pallas_call(
        functools.partial(
            project_kernel, (groups, counts, depth), has_start, widths
        ),
        out_shape=out_shape,
        grid_spec=pltpu.PrefetchScalarGridSpec(
            num_scalar_prefetch=1,
            grid=(1,),
            in_specs=in_specs,
            out_specs=[pl.BlockSpec(memory_space=pltpu.VMEM)] * len(out_shape),
            scratch_shapes=[
                pltpu.VMEM((groups // per, rows, per * depth), jnp.bfloat16),
                pltpu.VMEM((groups // per, per * depth, columns), jnp.bfloat16),
                pltpu.VMEM((rows, columns), jnp.float32),
                pltpu.SemaphoreType.DMA((groups // per, copies)),
            ],
        ),
        compiler_params=pltpu.CompilerParams(
            dimension_semantics=("arbitrary",), vmem_limit_bytes=40 * MIB
        ),
        cost_estimate=pl.CostEstimate(
            flops=2 * rows * depth * groups * columns,
            bytes_accessed=2 * groups * depth * (rows + columns) + 4 * rows * columns,
            transcendentals=0,
        ),
        name="project",
    )(ids, *operands)


def pack_kernel(reqs, first_pos, live_ref, kv_ref, *refs):
    out_ref = refs[-1]
    dests, length, columns = out_ref.shape
    each = kv_ref.shape[0] // reqs // 16 * 16
    block = each // dests
    pos = first_pos + lax.broadcasted_iota(jnp.int32, (each, 1), 0)
    for req in range(reqs):
        rows = kv_ref[req * each : (req + 1) * each, :]
        rows = jnp.where(pos < live_ref[req], rows, jnp.zeros_like(rows))
        for dest in range(dests):
            out_ref[dest, req * block : (req + 1) * block, :] = rows[
                dest * block : (dest + 1) * block
            ]
    if len(refs) == 1:
        return
    q_ref = refs[0]
    count = length - reqs * block
    per = q_ref.shape[1] // columns + 1
    at = reqs * each
    queries = q_ref[...].astype(jnp.float32)
    keyvals = kv_ref[at : at + q_ref.shape[0], :].astype(jnp.float32)
    slab = []
    for row in range(count // per):
        for part in range(per - 1):
            slab.append(queries[row : row + 1, part * columns : (part + 1) * columns])
        slab.append(keyvals[row : row + 1, :])
    slab = jnp.concatenate(slab, axis=0).astype(jnp.bfloat16)
    for dest in range(dests):
        out_ref[dest, reqs * block :, :] = slab


def pack(keyvals, reqs, first_pos, lives, dests, queries=None):
    columns = keyvals.shape[1]
    each = keyvals.shape[0] // reqs // 16 * 16
    length = reqs * each // dests
    operands = [keyvals]
    in_specs = [pl.BlockSpec(memory_space=pltpu.VMEM)]
    if queries is not None:
        length += reqs * STEPS * (queries.shape[1] // columns + 1)
        operands.append(queries)
        row = reqs * each // DEC_ROWS
        in_specs.append(pl.BlockSpec((DEC_ROWS, queries.shape[1]), lambda *_: (row, 0)))
    return pl.pallas_call(
        functools.partial(pack_kernel, reqs, first_pos),
        out_shape=jax.ShapeDtypeStruct((dests, length, columns), keyvals.dtype),
        grid_spec=pltpu.PrefetchScalarGridSpec(
            num_scalar_prefetch=1,
            grid=(1,),
            in_specs=in_specs,
            out_specs=pl.BlockSpec(memory_space=pltpu.VMEM),
        ),
        compiler_params=pltpu.CompilerParams(vmem_limit_bytes=16 * MIB),
        cost_estimate=pl.CostEstimate(
            flops=0, bytes_accessed=4 * dests * length * columns, transcendentals=0
        ),
        name="pack",
    )(lives, *operands)


def route_kernel(block, count, source, *refs):
    got_refs, out_ref = refs[:count], refs[-1]
    dests = out_ref.shape[0]
    per_rep = source.shape[0] // dests
    for slot in range(source.shape[0]):
        request = source[slot]
        at = pl.ds(pl.multiple_of((request % per_rep) * block, block), block)
        for part in range(count):
            low = (part * per_rep + slot % per_rep) * block
            out_ref[slot // per_rep, low : low + block, :] = got_refs[part][
                request // per_rep, at, :
            ]
    low = count * per_rep * block
    for extra_ref in refs[count:-1]:
        for dest in range(dests):
            out_ref[dest, low : low + extra_ref.shape[0], :] = extra_ref[...]


def route(got, source, block, *extra):
    dests, _, columns = got[0].shape
    per_rep = source.shape[0] // dests
    length = len(got) * per_rep * block + sum(x.shape[0] for x in extra)
    operands = [*got, *extra]
    return pl.pallas_call(
        functools.partial(route_kernel, block, len(got)),
        out_shape=jax.ShapeDtypeStruct((dests, length, columns), got[0].dtype),
        grid_spec=pltpu.PrefetchScalarGridSpec(
            num_scalar_prefetch=1,
            grid=(1,),
            in_specs=[pl.BlockSpec(memory_space=pltpu.VMEM)] * len(operands),
            out_specs=pl.BlockSpec(memory_space=pltpu.VMEM),
        ),
        compiler_params=pltpu.CompilerParams(vmem_limit_bytes=16 * MIB),
        cost_estimate=pl.CostEstimate(
            flops=0, bytes_accessed=4 * dests * length * columns, transcendentals=0
        ),
        name="route",
    )(source, *operands)


def finish_kernel(block, count, source, home_ref, earlier_ref, cache_ref, out_ref):
    dests, _, columns = home_ref.shape
    per_rep = out_ref.shape[0] // STEPS
    slot = pl.program_id(0)
    for part in range(count):
        at = pl.ds(pl.multiple_of((part * per_rep + slot) * block, block), block)
        for dest in range(dests):
            low = (part * dests + dest) * block
            cache_ref[0, low : low + block, :] = home_ref[dest, at, :]

    @pl.when(slot == 0)
    def _():
        low = count * per_rep * block
        for mine in range(per_rep):
            request = source[mine]
            both = home_ref[request // per_rep, low : low + 16, :].astype(jnp.float32)
            rows = jnp.where(request % per_rep == 0, both[:8], both[8:])
            for step in range(STEPS):
                for part in range(out_ref.shape[1] // columns):
                    row = step * (8 // STEPS) + part
                    at = mine * STEPS + step
                    out_ref[at : at + 1, part * columns : (part + 1) * columns] = rows[
                        row : row + 1
                    ].astype(jnp.bfloat16)


def finish(home, earlier, source, block, count, q_cols):
    dests, _, columns = home.shape
    per_rep, total_len, _ = earlier.shape
    new_len = count * dests * block
    return pl.pallas_call(
        functools.partial(finish_kernel, block, count),
        out_shape=(
            jax.ShapeDtypeStruct(earlier.shape, earlier.dtype),
            jax.ShapeDtypeStruct((per_rep * STEPS, q_cols), earlier.dtype),
        ),
        grid_spec=pltpu.PrefetchScalarGridSpec(
            num_scalar_prefetch=1,
            grid=(per_rep,),
            in_specs=[
                pl.BlockSpec(memory_space=pltpu.VMEM),
                pl.BlockSpec(memory_space=pltpu.HBM),
            ],
            out_specs=(
                pl.BlockSpec((1, new_len, columns), lambda c, *_: (c, total_len // new_len - 1, 0)),
                pl.BlockSpec(memory_space=pltpu.VMEM),
            ),
        ),
        input_output_aliases={2: 0},
        compiler_params=pltpu.CompilerParams(vmem_limit_bytes=16 * MIB),
        name="finish",
    )(source, home, earlier)


def phase_end(*arrays):
    return lax.optimization_barrier(arrays)


def prefill_kernel(parts, ctx_len, fill_ref, live_ref, q_ref, prefix_ref, *refs):
    kv_refs = refs[: parts + 1]
    out_ref = refs[-1]
    req = pl.program_id(0)
    fill = fill_ref[req]
    live = live_ref[req]
    rows = q_ref.shape[0]
    first_row = parts * rows
    row_ids = lax.broadcasted_iota(jnp.int32, (rows, 1), 0)
    own_ids = lax.broadcasted_iota(jnp.int32, (rows, rows), 1)
    causal = own_ids <= lax.broadcasted_iota(jnp.int32, (rows, rows), 0)

    def heads(blocks):
        seen = blocks * KEY_BLOCK
        last = seen - KEY_BLOCK
        last_live = last + lax.broadcasted_iota(jnp.int32, (rows, KEY_BLOCK), 1) < fill

        def one_head(h):
            cols = pl.ds(pl.multiple_of(h * HD, HD), HD)
            query = q_ref[:, cols]
            scores = []
            if last:
                scores.append(dot_nt(query, prefix_ref[0, :last, :HD]))
            scores.append(
                jnp.where(last_live, dot_nt(query, prefix_ref[0, last:seen, :HD]), LOW_SCORE)
            )
            for part in range(parts):
                scores.append(dot_nt(query, kv_refs[part][:, :HD]))
            scores.append(jnp.where(causal, dot_nt(query, kv_refs[parts][:, :HD]), LOW_SCORE))
            top = scores[0].max(axis=1, keepdims=True)
            for score in scores[1:]:
                top = jnp.maximum(top, score.max(axis=1, keepdims=True))
            weights = [jnp.exp2((score - top) * EXP_SCALE) for score in scores]
            total = weights[0].sum(axis=1, keepdims=True)
            for weight in weights[1:]:
                total = total + weight.sum(axis=1, keepdims=True)
            weights = [weight.astype(jnp.bfloat16) for weight in weights]
            mixed = None
            values = []
            if last:
                values.append(prefix_ref[0, :last, HD:])
            values.append(prefix_ref[0, last:seen, HD:])
            for part in range(parts + 1):
                values.append(kv_refs[part][:, HD:])
            for weight, value in zip(weights, values):
                term = dot_nn(weight, value)
                mixed = term if mixed is None else mixed + term
            mixed = mixed / total
            if parts:
                mixed = jnp.where(first_row + row_ids < live, mixed, 0.0)
            out_ref[:, cols] = mixed.astype(jnp.bfloat16)

        @pl.loop(0, GROUP // 2)
        def _(pair):
            one_head(2 * pair)
            one_head(2 * pair + 1)

    block_count = (fill + KEY_BLOCK - 1) // KEY_BLOCK
    is_live = first_row < live
    for blocks in range(1, ctx_len // KEY_BLOCK + 1):

        @pl.when((block_count == blocks) & is_live)
        def _(blocks=blocks):
            heads(blocks)

    @pl.when(jnp.logical_not(is_live))
    def _():
        out_ref[...] = jnp.zeros_like(out_ref)


def prefill_part(part, part_count, queries, prefix, keyvals, fills, lives, earlier_out):
    cols = queries.shape[1]
    reqs, ctx_len, pair_cols = prefix.shape
    rows = queries.shape[0] // reqs // 16 * 16
    in_specs = [
        pl.BlockSpec((rows, cols), lambda r, *_: (r, 0)),
        pl.BlockSpec((1, ctx_len, pair_cols), lambda r, *_: (r, 0, 0)),
    ]
    in_specs += [pl.BlockSpec((rows, pair_cols), lambda r, *_: (r, 0))] * (part + 1)
    operands = [queries, prefix, *keyvals[: part + 1]]
    aliases = {}
    if earlier_out is not None:
        in_specs.append(pl.BlockSpec(memory_space=pl.ANY))
        aliases = {2 + len(operands): 0}
        operands.append(earlier_out)
    return pl.pallas_call(
        functools.partial(prefill_kernel, part, ctx_len),
        out_shape=jax.ShapeDtypeStruct((reqs * part_count * rows, cols), jnp.bfloat16),
        grid_spec=pltpu.PrefetchScalarGridSpec(
            num_scalar_prefetch=2,
            grid=(reqs,),
            in_specs=in_specs,
            out_specs=pl.BlockSpec((rows, cols), lambda r, *_: (r * part_count + part, 0)),
        ),
        input_output_aliases=aliases,
        compiler_params=pltpu.CompilerParams(
            dimension_semantics=("arbitrary",), vmem_limit_bytes=24 * MIB
        ),
        cost_estimate=pl.CostEstimate(
            flops=4 * reqs * rows * cols * (ctx_len + rows),
            bytes_accessed=2 * reqs * (2 * rows * cols + ctx_len * pair_cols),
            transcendentals=reqs * rows * (cols // HD) * (ctx_len + rows),
        ),
        name="prefill",
    )(fills, lives, *operands)


def decode_kernel(parts, held, owner_ref, fill_ref, live_ref, got_ref, prefix_ref, *refs):
    kv_refs = refs[:parts]
    out_ref = refs[-1]
    reqs = prefix_ref.shape[0]
    ctx_len = prefix_ref.shape[1]
    part_len = kv_refs[0].shape[0] // reqs // 16 * 16
    half = out_ref.shape[0] // reqs

    def live_where(count, limit, scores):
        return jnp.where(
            lax.broadcasted_iota(jnp.int32, scores.shape, 1) < limit, scores, LOW_SCORE
        )

    for req in range(reqs):
        slot = owner_ref[req]
        fill = fill_ref[req]
        live = live_ref[req]
        both = got_ref[slot // reqs, held : held + 2 * half, :].astype(jnp.float32)
        slab = jnp.where(slot % reqs == 0, both[:half], both[half:])
        query = jnp.concatenate([slab[:, :HD], slab[:, HD:]], axis=0).astype(jnp.bfloat16)
        rows = query.shape[0]
        scores = [live_where(ctx_len, fill, dot_nt(query, prefix_ref[req, :, :HD]))]
        values = [prefix_ref[req, :, HD:]]
        for part in range(parts):
            part_scores = dot_nt(query, kv_refs[part][req * part_len : (req + 1) * part_len, :HD])
            scores.append(live_where(part_len, live - part * part_len, part_scores))
            values.append(kv_refs[part][req * part_len : (req + 1) * part_len, HD:])
        own_scores = dot_nt(query, query)
        row_ids = lax.broadcasted_iota(jnp.int32, own_scores.shape, 0)
        key_ids = lax.broadcasted_iota(jnp.int32, own_scores.shape, 1)
        per_step = half // STEPS
        is_key = (key_ids < half) & (key_ids % per_step == per_step - 1)
        seen = key_ids // per_step <= row_ids % half // per_step
        scores.append(jnp.where(is_key & seen, own_scores, LOW_SCORE))
        own_values = slab[:, HD:].astype(jnp.bfloat16)
        values.append(jnp.concatenate([own_values, own_values], axis=0))
        top = scores[0].max(axis=1, keepdims=True)
        for score in scores[1:]:
            top = jnp.maximum(top, score.max(axis=1, keepdims=True))
        total = jnp.zeros((rows, 1), jnp.float32)
        mixed = jnp.zeros((rows, HD), jnp.float32)
        for score, value in zip(scores, values):
            weight = jnp.exp2((score - top) * EXP_SCALE)
            total = total + weight.sum(axis=1, keepdims=True)
            coarse = weight.astype(jnp.bfloat16)
            fine = (weight - coarse.astype(jnp.float32)).astype(jnp.bfloat16)
            mixed = mixed + dot_nn(coarse, value) + dot_nn(fine, value)
        mixed = mixed / total
        out_ref[req * half : (req + 1) * half, :HD] = mixed[:half].astype(jnp.bfloat16)
        out_ref[req * half : (req + 1) * half, HD:] = mixed[half:].astype(jnp.bfloat16)


def decode_part(got, held, prefix, keyvals, owners, fills, lives):
    reqs = prefix.shape[0]
    blocks = [got, prefix, *keyvals]
    slab = reqs * STEPS * (GROUP // 2 + 1)
    return pl.pallas_call(
        functools.partial(decode_kernel, len(keyvals), held),
        out_shape=jax.ShapeDtypeStruct((slab, got.shape[2]), jnp.bfloat16),
        grid_spec=pltpu.PrefetchScalarGridSpec(
            num_scalar_prefetch=3,
            grid=(1,),
            in_specs=[pl.BlockSpec(memory_space=pltpu.VMEM) for _ in blocks],
            out_specs=pl.BlockSpec(memory_space=pltpu.VMEM),
        ),
        compiler_params=pltpu.CompilerParams(
            dimension_semantics=("arbitrary",), vmem_limit_bytes=16 * MIB
        ),
        cost_estimate=pl.CostEstimate(
            flops=6 * slab * HD * 1536,
            bytes_accessed=2 * reqs * 1536 * 2 * HD,
            transcendentals=slab * 1536,
        ),
        name="decode",
    )(owners, fills, lives, *blocks)


def local(prompt, dec_tokens, w_query, w_keyval, prefix_cache, prompt_len, fill_len, owner):
    replicas = lax.axis_size("replica")
    tensors = lax.axis_size("tensor")
    ring = tensors // 2
    replica_id = lax.axis_index("replica")
    tensor_id = lax.axis_index("tensor")
    per_rep, ctx_len, pair_cols = prefix_cache.shape
    new_len = prompt.shape[0] // per_rep
    depth = prompt.shape[1]
    q_cols = w_query.shape[1]
    half = new_len // 2
    request_count = per_rep * replicas
    first_req = replica_id * per_rep

    def moved(plane, shift):
        return [
            (p * ring + y, ((p + plane) % 2) * ring + (y + shift) % ring)
            for p in range(2)
            for y in range(ring)
        ]

    def send(x, plane, shift):
        return lax.ppermute(x, "tensor", moved(plane, shift))

    my_plane, my_y = tensor_id // ring, tensor_id % ring

    def block_id(plane, shift):
        return ((my_plane + plane) % 2) * ring + (my_y + shift + ring) % ring

    ids = jnp.stack(
        [
            block_id(0, 0),
            block_id(1, 0),
            block_id(0, -1),
            block_id(0, 1),
            block_id(0, 2),
            block_id(1, -1),
            block_id(1, 1),
            block_id(1, 2),
        ]
    ).astype(jnp.int32)

    slot_ids = jnp.arange(request_count, dtype=jnp.int32)
    source = jnp.sum(jnp.where(owner[None, :] == slot_ids[:, None], slot_ids[None, :], 0), axis=1)
    fills = lax.dynamic_slice_in_dim(fill_len, first_req, per_rep, 0)
    lives = lax.dynamic_slice_in_dim(prompt_len, first_req, per_rep, 0)
    my_owner = lax.dynamic_slice_in_dim(owner, first_req, per_rep, 0)
    my_source = lax.dynamic_slice_in_dim(source, first_req, per_rep, 0)

    def exchange(x):
        return lax.all_to_all(x, "replica", split_axis=0, concat_axis=0, tiled=True)

    def zero_dead(x, first_pos, counts):
        pos = first_pos + jnp.arange(x.shape[1], dtype=jnp.int32)
        return jnp.where((pos[None, :] < counts[:, None])[:, :, None], x, jnp.zeros((), x.dtype))

    def for_spread(x):
        block = x.shape[1] // replicas
        return x.reshape(per_rep, replicas, block, pair_cols).transpose(1, 0, 2, 3).reshape(
            replicas, per_rep * block, pair_cols
        )

    def settled(x):
        block = x.shape[1] // per_rep
        return x.reshape(replicas, per_rep, block, pair_cols).transpose(1, 0, 2, 3).reshape(
            per_rep, replicas * block, pair_cols
        )

    rows = per_rep * half
    both = [w_query, w_keyval]
    block = half // replicas
    held = per_rep * block
    dec_pad = jnp.pad(dec_tokens, ((0, DEC_ROWS - dec_tokens.shape[0]), (0, 0)))
    by_req = prompt.reshape(per_rep, 2, half, depth)
    first = jnp.concatenate([by_req[:, 0].reshape(rows, depth), dec_pad], axis=0)
    second = by_req[:, 1].reshape(rows, depth)

    up0, down0, across0 = send(first, 0, 1), send(first, 0, -1), send(first, 1, 0)
    up1, down1, across1 = send(second, 0, 1), send(second, 0, -1), send(second, 1, 0)
    prefix_sent = for_spread(zero_dead(prefix_cache, 0, fills))
    up0, down0, across0, up1, down1, across1, prefix_sent = phase_end(
        up0, down0, across0, up1, down1, across1, prefix_sent
    )

    far0 = send(up0, 0, 1)
    far1 = send(down1, 0, -1)
    prefix_got = exchange(prefix_sent)
    early0 = project(
        [[first], [across0], [up0], [down0]], ids[:4], both, out_type=jnp.float32
    )[0]
    far0, far1, across0, across1, early0 = phase_end(far0, far1, across0, across1, early0)

    across_up0, across_down0 = send(across0, 0, 1), send(across0, 0, -1)
    across_far0 = send(far0, 1, 0)
    early1 = project(
        [[second], [across1], [up1], [down1]], ids[:4], both, out_type=jnp.float32
    )[0]
    prefix_sent = route([prefix_got], source, ctx_len // replicas)
    across_up0, across_down0, across_far0, across1, far1, prefix_sent, early1 = phase_end(
        across_up0, across_down0, across_far0, across1, far1, prefix_sent, early1
    )

    across_up1, across_down1 = send(across1, 0, 1), send(across1, 0, -1)
    across_far1 = send(far1, 1, 0)
    q0, kv0 = project(
        [[far0], [across_up0], [across_down0], [across_far0]], ids[4:], both, start=early0
    )
    got0 = exchange(pack(kv0, per_rep, 0, lives, replicas, q0))
    out0 = prefill_part(0, 2, q0, prefix_cache, [kv0], fills, lives, None)
    prefix_home = settled(exchange(prefix_sent))
    earlier = jnp.pad(prefix_home, ((0, 0), (0, new_len), (0, 0)))
    across_up1, across_down1, across_far1, got0, out0, kv0, earlier = phase_end(
        across_up1, across_down1, across_far1, got0, out0, kv0, earlier
    )

    late1 = [[far1], [across_up1], [across_down1], [across_far1]]
    kv1 = project(late1, ids[4:], [w_keyval], start=early1, start_col=q_cols)[0]
    got1 = exchange(pack(kv1, per_rep, half, lives, replicas))
    dec_back = decode_part(got0, held, prefix_cache, [kv0, kv1], my_owner, fills, lives)
    home = exchange(route([got0, got1], source, block, dec_back))
    decode_cache, decode_out = finish(home, earlier, my_source, block, 2, q_cols)

    q1 = project(late1, ids[4:], [w_query], start=early1)[0]
    prefill_out = prefill_part(1, 2, q1, prefix_cache, [kv0, kv1], fills, lives, out0)
    return (prefill_out, decode_out, decode_cache)


def solution(mesh):
    in_specs = (
        P("replica", "tensor"),
        P("replica", "tensor"),
        P(None, "tensor"),
        P(None, "tensor"),
        P("replica", None, "tensor"),
        P(),
        P(),
        P(),
    )
    out_specs = (P("replica", "tensor"), P("replica", "tensor"), P("replica", None, "tensor"))
    return jax.shard_map(local, mesh=mesh, in_specs=in_specs, out_specs=out_specs, check_vma=False)
```

```python
import functools
import math

import jax
import jax.numpy as jnp
from jax import lax
from jax.experimental import pallas as pl
from jax.experimental.pallas import tpu as pltpu
from jax.sharding import PartitionSpec as P

HEADS = 48
KV = 8
HD = 128
GROUP = HEADS // KV
STEPS = 2
DEC_ROWS = 16
KEY_BLOCK = 256
SMALL_VMEM = 16 * 1024 * 1024
WHOLE_VMEM = 62 * 1024 * 1024

LOW_SCORE = -1e30
EXP_SCALE = math.log2(math.e) / math.sqrt(HD)


def dot_nt(a, b):
    return lax.dot_general(a, b, (((1,), (1,)), ((), ())), preferred_element_type=jnp.float32)


def dot_nn(a, b):
    return lax.dot_general(a, b, (((1,), (0,)), ((), ())), preferred_element_type=jnp.float32)


def row_tiles(counts):
    tiles = []
    start = 0
    for count in counts:
        first = (count // 2 + 15) // 16 * 16
        tiles += [(start, first), (start + first, count - first)]
        start += count
    return tiles


def project_kernel(shape, has_start, start_col, spread, widths, ids, lives, *refs):
    groups, counts, depth = shape
    refs = list(refs)
    pieces = [[refs.pop(0) for _ in counts] for _ in range(groups)]
    weights = [refs.pop(0) for _ in widths]
    start_ref = refs.pop(0) if has_start else None
    held, weight_held, total, sems = refs[-4:]
    outs = refs[:-4]
    offsets = [sum(counts[:i]) for i in range(len(counts))]
    columns = [sum(widths[:i]) for i in range(len(widths))]
    per = 1

    def copies(k):
        made = []
        for j in range(k * per, (k + 1) * per):
            at = pl.ds((j - k * per) * depth, depth)
            for i, count in enumerate(counts):
                made.append((pieces[j][i], held.at[k, pl.ds(offsets[i], count), at]))
            half = depth // 2
            for i, width in enumerate(widths):
                for part in range(2):
                    src = pl.ds(pl.multiple_of(ids[j] * depth + part * half, half), half)
                    dst = pl.ds((j - k * per) * depth + part * half, half)
                    made.append(
                        (
                            weights[i].at[src, :],
                            weight_held.at[k, dst, pl.ds(columns[i], width)],
                        )
                    )
        return [
            pltpu.make_async_copy(src, dst, sems.at[k, n]) for n, (src, dst) in enumerate(made)
        ]

    steps = groups // per
    all_columns = sum(widths)
    for copy in copies(0):
        copy.start()
    if has_start:
        before = pltpu.make_async_copy(
            start_ref.at[:, pl.ds(start_col, all_columns)], total, sems.at[steps, 0]
        )
        before.start()
    for k in range(1, steps):
        for copy in copies(k):
            copy.start()
    for k in range(steps):
        for copy in copies(k):
            copy.wait()
        if k == 0 and has_start:
            before.wait()
        for row, count in row_tiles(counts):
            for col in range(0, all_columns, 512):
                width = min(512, all_columns - col)
                at = (slice(row, row + count), slice(col, col + width))
                part = dot_nn(held[k, row : row + count, :], weight_held[k, :, col : col + width])
                if k or has_start:
                    part = part + total[at]
                if k < steps - 1:
                    total[at] = part
                    continue
                if outs[0].dtype == jnp.float32:
                    group = max(i for i, offset in enumerate(offsets) if offset <= row)
                    low = row - offsets[group]
                    outs[group][low : low + count, col : col + width] = part
                    continue
                for out, first, wide in zip(outs[: len(widths)], columns, widths):
                    low, high = max(first, col), min(first + wide, col + width)
                    if low < high:
                        value = part[:, low - col : high - col].astype(jnp.bfloat16)
                        out[row : row + count, low - first : high - first] = value
    if spread:
        pack(spread, lives, outs)


def pack(spread, lives, outs):
    reqs, first_pos, dests, _ = spread
    q_ref, kv_ref, spread_ref = outs[0], outs[-2], outs[-1]
    columns = kv_ref.shape[1]
    each = kv_ref.shape[0] // reqs // 16 * 16
    block = each // dests
    pos = first_pos + lax.broadcasted_iota(jnp.int32, (each, 1), 0)
    for req in range(reqs):
        rows = kv_ref[req * each : (req + 1) * each, :]
        rows = jnp.where(pos < lives[req], rows, jnp.zeros_like(rows))
        for dest in range(dests):
            spread_ref[dest, req * block : (req + 1) * block, :] = rows[
                dest * block : (dest + 1) * block
            ]
    if spread_ref.shape[1] == reqs * block:
        return
    queries = q_ref[reqs * each :, :].astype(jnp.float32)
    keyvals = kv_ref[reqs * each :, :].astype(jnp.float32)
    slab = []
    for row in range(reqs * STEPS):
        for low in range(0, queries.shape[1], columns):
            slab.append(queries[row : row + 1, low : low + columns])
        slab.append(keyvals[row : row + 1, :])
    slab = jnp.concatenate(slab, axis=0).astype(jnp.bfloat16)
    for dest in range(dests):
        spread_ref[dest, reqs * block :, :] = slab


def project(pieces, ids, weights, lives, start=None, start_col=0, out_type=jnp.bfloat16, spread=None):
    groups = len(pieces)
    counts = tuple(x.shape[0] for x in pieces[0])
    depth = pieces[0][0].shape[1]
    widths = tuple(w.shape[1] for w in weights)
    rows, columns = sum(counts), sum(widths)
    has_start = start is not None
    operands = [x for group in pieces for x in group] + list(weights)
    in_specs = [pl.BlockSpec(memory_space=pltpu.HBM)] * len(operands)
    if has_start:
        in_specs.append(pl.BlockSpec(memory_space=pltpu.HBM))
        operands.append(start)
    if out_type == jnp.float32:
        out_shape = [jax.ShapeDtypeStruct((count, columns), jnp.float32) for count in counts]
    else:
        out_shape = [jax.ShapeDtypeStruct((rows, w), jnp.bfloat16) for w in widths]
    if spread:
        reqs, _, dests, has_dec = spread
        length = rows // reqs // 16 * 16 * reqs // dests
        if has_dec:
            length += reqs * STEPS * (widths[0] // widths[-1] + 1)
        out_shape.append(jax.ShapeDtypeStruct((dests, length, widths[-1]), jnp.bfloat16))
    per = 1
    copies = per * (len(counts) + 2 * len(widths))
    return pl.pallas_call(
        functools.partial(
            project_kernel, (groups, counts, depth), has_start, start_col, spread, widths
        ),
        out_shape=out_shape,
        grid_spec=pltpu.PrefetchScalarGridSpec(
            num_scalar_prefetch=2,
            grid=(1,),
            in_specs=in_specs,
            out_specs=[pl.BlockSpec(memory_space=pltpu.VMEM)] * len(out_shape),
            scratch_shapes=[
                pltpu.VMEM((groups // per, rows, per * depth), jnp.bfloat16),
                pltpu.VMEM((groups // per, per * depth, columns), jnp.bfloat16),
                pltpu.VMEM((rows, columns), jnp.float32),
                pltpu.SemaphoreType.DMA((groups // per + 1, copies)),
            ],
        ),
        compiler_params=pltpu.CompilerParams(
            dimension_semantics=("arbitrary",), vmem_limit_bytes=WHOLE_VMEM
        ),
        cost_estimate=pl.CostEstimate(
            flops=2 * rows * depth * groups * columns,
            bytes_accessed=2 * groups * depth * (rows + columns) + 4 * rows * columns,
            transcendentals=0,
        ),
        name="project",
    )(ids, lives, *operands)


def route_kernel(block, count, source, *refs):
    got_refs, out_ref = refs[:count], refs[-1]
    dests = out_ref.shape[0]
    per_rep = source.shape[0] // dests
    for slot in range(source.shape[0]):
        request = source[slot]
        at = pl.ds(pl.multiple_of((request % per_rep) * block, block), block)
        for part in range(count):
            low = (part * per_rep + slot % per_rep) * block
            out_ref[slot // per_rep, low : low + block, :] = got_refs[part][
                request // per_rep, at, :
            ]
    low = count * per_rep * block
    for extra_ref in refs[count:-1]:
        for dest in range(dests):
            out_ref[dest, low : low + extra_ref.shape[0], :] = extra_ref[...]


def route(got, source, block, *extra):
    dests, _, columns = got[0].shape
    per_rep = source.shape[0] // dests
    length = len(got) * per_rep * block + sum(x.shape[0] for x in extra)
    operands = [*got, *extra]
    return pl.pallas_call(
        functools.partial(route_kernel, block, len(got)),
        out_shape=jax.ShapeDtypeStruct((dests, length, columns), got[0].dtype),
        grid_spec=pltpu.PrefetchScalarGridSpec(
            num_scalar_prefetch=1,
            grid=(1,),
            in_specs=[pl.BlockSpec(memory_space=pltpu.VMEM)] * len(operands),
            out_specs=pl.BlockSpec(memory_space=pltpu.VMEM),
        ),
        compiler_params=pltpu.CompilerParams(vmem_limit_bytes=SMALL_VMEM),
        cost_estimate=pl.CostEstimate(
            flops=0, bytes_accessed=4 * dests * length * columns, transcendentals=0
        ),
        name="route",
    )(source, *operands)


def settle_kernel(got_ref, out_ref):
    dests, length, _ = got_ref.shape
    block = out_ref.shape[1] // dests
    at = pl.ds(pl.multiple_of(pl.program_id(0) * block, block), block)
    for dest in range(dests):
        out_ref[0, dest * block : (dest + 1) * block, :] = got_ref[dest, at, :]


def settle(got, per_rep, total_len):
    dests, length, columns = got.shape
    held = dests * length // per_rep
    return pl.pallas_call(
        settle_kernel,
        out_shape=jax.ShapeDtypeStruct((per_rep, total_len, columns), got.dtype),
        grid=(per_rep,),
        in_specs=[pl.BlockSpec(memory_space=pltpu.VMEM)],
        out_specs=pl.BlockSpec((1, held, columns), lambda c: (c, 0, 0)),
        compiler_params=pltpu.CompilerParams(vmem_limit_bytes=SMALL_VMEM),
        name="settle",
    )(got)


def finish_kernel(block, count, source, home_ref, earlier_ref, cache_ref, out_ref):
    dests, _, columns = home_ref.shape
    per_rep = out_ref.shape[0] // STEPS
    slot = pl.program_id(0)
    for part in range(count):
        at = pl.ds(pl.multiple_of((part * per_rep + slot) * block, block), block)
        for dest in range(dests):
            low = (part * dests + dest) * block
            cache_ref[0, low : low + block, :] = home_ref[dest, at, :]

    @pl.when(slot == 0)
    def _():
        low = count * per_rep * block
        for mine in range(per_rep):
            request = source[mine]
            both = home_ref[request // per_rep, low : low + 16, :].astype(jnp.float32)
            rows = jnp.where(request % per_rep == 0, both[:8], both[8:])
            for step in range(STEPS):
                for part in range(out_ref.shape[1] // columns):
                    row = step * (8 // STEPS) + part
                    at = mine * STEPS + step
                    out_ref[at : at + 1, part * columns : (part + 1) * columns] = rows[
                        row : row + 1
                    ].astype(jnp.bfloat16)


def finish(home, earlier, source, block, count, q_cols):
    dests, _, columns = home.shape
    per_rep, total_len, _ = earlier.shape
    new_len = count * dests * block
    return pl.pallas_call(
        functools.partial(finish_kernel, block, count),
        out_shape=(
            jax.ShapeDtypeStruct(earlier.shape, earlier.dtype),
            jax.ShapeDtypeStruct((per_rep * STEPS, q_cols), earlier.dtype),
        ),
        grid_spec=pltpu.PrefetchScalarGridSpec(
            num_scalar_prefetch=1,
            grid=(per_rep,),
            in_specs=[
                pl.BlockSpec(memory_space=pltpu.VMEM),
                pl.BlockSpec(memory_space=pltpu.HBM),
            ],
            out_specs=(
                pl.BlockSpec((1, new_len, columns), lambda c, *_: (c, total_len // new_len - 1, 0)),
                pl.BlockSpec(memory_space=pltpu.VMEM),
            ),
        ),
        input_output_aliases={2: 0},
        compiler_params=pltpu.CompilerParams(vmem_limit_bytes=SMALL_VMEM),
        name="finish",
    )(source, home, earlier)


def phase_end(*arrays):
    return lax.optimization_barrier(arrays)


def prefill_kernel(parts, ctx_len, fill_ref, live_ref, q_ref, prefix_ref, *refs):
    kv_refs = refs[: parts + 1]
    out_ref = refs[-1]
    req = pl.program_id(0)
    fill = fill_ref[req]
    live = live_ref[req]
    rows = q_ref.shape[0]
    first_row = parts * rows
    row_ids = lax.broadcasted_iota(jnp.int32, (rows, 1), 0)
    own_ids = lax.broadcasted_iota(jnp.int32, (rows, rows), 1)
    causal = own_ids <= lax.broadcasted_iota(jnp.int32, (rows, rows), 0)

    def heads(blocks):
        seen = blocks * KEY_BLOCK
        last = seen - KEY_BLOCK
        last_live = last + lax.broadcasted_iota(jnp.int32, (rows, KEY_BLOCK), 1) < fill

        def one_head(h):
            cols = pl.ds(pl.multiple_of(h * HD, HD), HD)
            query = q_ref[:, cols]
            scores = []
            if last:
                scores.append(dot_nt(query, prefix_ref[0, :last, :HD]))
            scores.append(
                jnp.where(last_live, dot_nt(query, prefix_ref[0, last:seen, :HD]), LOW_SCORE)
            )
            for part in range(parts):
                scores.append(dot_nt(query, kv_refs[part][:, :HD]))
            scores.append(jnp.where(causal, dot_nt(query, kv_refs[parts][:, :HD]), LOW_SCORE))
            top = scores[0].max(axis=1, keepdims=True)
            for score in scores[1:]:
                top = jnp.maximum(top, score.max(axis=1, keepdims=True))
            weights = [jnp.exp2((score - top) * EXP_SCALE) for score in scores]
            total = weights[0].sum(axis=1, keepdims=True)
            for weight in weights[1:]:
                total = total + weight.sum(axis=1, keepdims=True)
            weights = [weight.astype(jnp.bfloat16) for weight in weights]
            mixed = None
            values = []
            if last:
                values.append(prefix_ref[0, :last, HD:])
            values.append(prefix_ref[0, last:seen, HD:])
            for part in range(parts + 1):
                values.append(kv_refs[part][:, HD:])
            for weight, value in zip(weights, values):
                term = dot_nn(weight, value)
                mixed = term if mixed is None else mixed + term
            mixed = mixed / total
            if parts:
                mixed = jnp.where(first_row + row_ids < live, mixed, 0.0)
            out_ref[:, cols] = mixed.astype(jnp.bfloat16)

        @pl.loop(0, GROUP // 3)
        def _(triple):
            for n in range(3):
                one_head(3 * triple + n)

    block_count = (fill + KEY_BLOCK - 1) // KEY_BLOCK
    is_live = first_row < live
    for blocks in range(1, ctx_len // KEY_BLOCK + 1):

        @pl.when((block_count == blocks) & is_live)
        def _(blocks=blocks):
            heads(blocks)

    @pl.when(jnp.logical_not(is_live))
    def _():
        out_ref[...] = jnp.zeros_like(out_ref)


def prefill_part(part, part_count, queries, prefix, keyvals, fills, lives, earlier_out):
    cols = queries.shape[1]
    reqs, ctx_len, pair_cols = prefix.shape
    rows = queries.shape[0] // reqs // 16 * 16
    in_specs = [
        pl.BlockSpec((rows, cols), lambda r, *_: (r, 0)),
        pl.BlockSpec((1, ctx_len, pair_cols), lambda r, *_: (r, 0, 0)),
    ]
    in_specs += [pl.BlockSpec((rows, pair_cols), lambda r, *_: (r, 0))] * (part + 1)
    operands = [queries, prefix, *keyvals[: part + 1]]
    aliases = {}
    if earlier_out is not None:
        in_specs.append(pl.BlockSpec(memory_space=pl.ANY))
        aliases = {2 + len(operands): 0}
        operands.append(earlier_out)
    return pl.pallas_call(
        functools.partial(prefill_kernel, part, ctx_len),
        out_shape=jax.ShapeDtypeStruct((reqs * part_count * rows, cols), jnp.bfloat16),
        grid_spec=pltpu.PrefetchScalarGridSpec(
            num_scalar_prefetch=2,
            grid=(reqs,),
            in_specs=in_specs,
            out_specs=pl.BlockSpec((rows, cols), lambda r, *_: (r * part_count + part, 0)),
        ),
        input_output_aliases=aliases,
        compiler_params=pltpu.CompilerParams(
            dimension_semantics=("arbitrary",), vmem_limit_bytes=WHOLE_VMEM
        ),
        cost_estimate=pl.CostEstimate(
            flops=4 * reqs * rows * cols * (ctx_len + rows),
            bytes_accessed=2 * reqs * (2 * rows * cols + ctx_len * pair_cols),
            transcendentals=reqs * rows * (cols // HD) * (ctx_len + rows),
        ),
        name="prefill",
    )(fills, lives, *operands)


def decode_kernel(parts, held, owner_ref, fill_ref, live_ref, got_ref, prefix_ref, *refs):
    kv_refs = refs[:parts]
    out_ref = refs[-1]
    reqs = prefix_ref.shape[0]
    ctx_len = prefix_ref.shape[1]
    part_len = kv_refs[0].shape[0] // reqs // 16 * 16
    half = out_ref.shape[0] // reqs

    def live_where(count, limit, scores):
        return jnp.where(
            lax.broadcasted_iota(jnp.int32, scores.shape, 1) < limit, scores, LOW_SCORE
        )

    for req in range(reqs):
        slot = owner_ref[req]
        fill = fill_ref[req]
        live = live_ref[req]
        both = got_ref[slot // reqs, held : held + 2 * half, :].astype(jnp.float32)
        slab = jnp.where(slot % reqs == 0, both[:half], both[half:])
        query = jnp.concatenate([slab[:, :HD], slab[:, HD:]], axis=0).astype(jnp.bfloat16)
        rows = query.shape[0]
        scores = [live_where(ctx_len, fill, dot_nt(query, prefix_ref[req, :, :HD]))]
        values = [prefix_ref[req, :, HD:]]
        for part in range(parts):
            part_scores = dot_nt(query, kv_refs[part][req * part_len : (req + 1) * part_len, :HD])
            scores.append(live_where(part_len, live - part * part_len, part_scores))
            values.append(kv_refs[part][req * part_len : (req + 1) * part_len, HD:])
        own_scores = dot_nt(query, query)
        row_ids = lax.broadcasted_iota(jnp.int32, own_scores.shape, 0)
        key_ids = lax.broadcasted_iota(jnp.int32, own_scores.shape, 1)
        per_step = half // STEPS
        is_key = (key_ids < half) & (key_ids % per_step == per_step - 1)
        seen = key_ids // per_step <= row_ids % half // per_step
        scores.append(jnp.where(is_key & seen, own_scores, LOW_SCORE))
        own_values = slab[:, HD:].astype(jnp.bfloat16)
        values.append(jnp.concatenate([own_values, own_values], axis=0))
        top = scores[0].max(axis=1, keepdims=True)
        for score in scores[1:]:
            top = jnp.maximum(top, score.max(axis=1, keepdims=True))
        total = jnp.zeros((rows, 1), jnp.float32)
        mixed = jnp.zeros((rows, HD), jnp.float32)
        for score, value in zip(scores, values):
            weight = jnp.exp2((score - top) * EXP_SCALE)
            total = total + weight.sum(axis=1, keepdims=True)
            coarse = weight.astype(jnp.bfloat16)
            fine = (weight - coarse.astype(jnp.float32)).astype(jnp.bfloat16)
            mixed = mixed + dot_nn(coarse, value) + dot_nn(fine, value)
        mixed = mixed / total
        out_ref[req * half : (req + 1) * half, :HD] = mixed[:half].astype(jnp.bfloat16)
        out_ref[req * half : (req + 1) * half, HD:] = mixed[half:].astype(jnp.bfloat16)


def decode_part(got, held, prefix, keyvals, owners, fills, lives):
    reqs = prefix.shape[0]
    blocks = [got, prefix, *keyvals]
    slab = reqs * STEPS * (GROUP // 2 + 1)
    return pl.pallas_call(
        functools.partial(decode_kernel, len(keyvals), held),
        out_shape=jax.ShapeDtypeStruct((slab, got.shape[2]), jnp.bfloat16),
        grid_spec=pltpu.PrefetchScalarGridSpec(
            num_scalar_prefetch=3,
            grid=(1,),
            in_specs=[pl.BlockSpec(memory_space=pltpu.VMEM) for _ in blocks],
            out_specs=pl.BlockSpec(memory_space=pltpu.VMEM),
        ),
        compiler_params=pltpu.CompilerParams(
            dimension_semantics=("arbitrary",), vmem_limit_bytes=WHOLE_VMEM
        ),
        cost_estimate=pl.CostEstimate(
            flops=6 * slab * HD * 1536,
            bytes_accessed=2 * reqs * 1536 * 2 * HD,
            transcendentals=slab * 1536,
        ),
        name="decode",
    )(owners, fills, lives, *blocks)


def local(prompt, dec_tokens, w_query, w_keyval, prefix_cache, prompt_len, fill_len, owner):
    replicas = lax.axis_size("replica")
    tensors = lax.axis_size("tensor")
    ring = tensors // 2
    replica_id = lax.axis_index("replica")
    tensor_id = lax.axis_index("tensor")
    per_rep, ctx_len, pair_cols = prefix_cache.shape
    new_len = prompt.shape[0] // per_rep
    depth = prompt.shape[1]
    q_cols = w_query.shape[1]
    half = new_len // 2
    request_count = per_rep * replicas
    first_req = replica_id * per_rep

    def moved(plane, shift):
        return [
            (p * ring + y, ((p + plane) % 2) * ring + (y + shift) % ring)
            for p in range(2)
            for y in range(ring)
        ]

    def send(x, plane, shift):
        return lax.ppermute(x, "tensor", moved(plane, shift))

    my_plane, my_y = tensor_id // ring, tensor_id % ring

    def block_id(plane, shift):
        return ((my_plane + plane) % 2) * ring + (my_y + shift + ring) % ring

    ids = jnp.stack(
        [
            block_id(0, 0),
            block_id(1, 0),
            block_id(0, -1),
            block_id(0, 1),
            block_id(0, 2),
            block_id(1, -1),
            block_id(1, 1),
            block_id(1, 2),
        ]
    ).astype(jnp.int32)

    slot_ids = jnp.arange(request_count, dtype=jnp.int32)
    source = jnp.sum(jnp.where(owner[None, :] == slot_ids[:, None], slot_ids[None, :], 0), axis=1)
    fills = lax.dynamic_slice_in_dim(fill_len, first_req, per_rep, 0)
    lives = lax.dynamic_slice_in_dim(prompt_len, first_req, per_rep, 0)
    my_owner = lax.dynamic_slice_in_dim(owner, first_req, per_rep, 0)
    my_source = lax.dynamic_slice_in_dim(source, first_req, per_rep, 0)

    def exchange(x):
        return lax.all_to_all(x, "replica", split_axis=0, concat_axis=0, tiled=True)

    def zero_dead(x, first_pos, counts):
        pos = first_pos + jnp.arange(x.shape[1], dtype=jnp.int32)
        return jnp.where((pos[None, :] < counts[:, None])[:, :, None], x, jnp.zeros((), x.dtype))

    def for_spread(x):
        block = x.shape[1] // replicas
        return x.reshape(per_rep, replicas, block, pair_cols).transpose(1, 0, 2, 3).reshape(
            replicas, per_rep * block, pair_cols
        )

    rows = per_rep * half
    both = [w_query, w_keyval]
    block = half // replicas
    held = per_rep * block
    dec_pad = jnp.pad(dec_tokens, ((0, DEC_ROWS - dec_tokens.shape[0]), (0, 0)))
    by_req = prompt.reshape(per_rep, 2, half, depth)
    first = jnp.concatenate([by_req[:, 0].reshape(rows, depth), dec_pad], axis=0)
    second = by_req[:, 1].reshape(rows, depth)

    up0, down0, across0 = send(first, 0, 1), send(first, 0, -1), send(first, 1, 0)
    up1, down1, across1 = send(second, 0, 1), send(second, 0, -1), send(second, 1, 0)
    prefix_got = exchange(for_spread(zero_dead(prefix_cache, 0, fills)))
    prefix_sent = route([prefix_got], source, ctx_len // replicas)
    early0 = project(
        [[first], [across0], [up0], [down0]], ids[:4], both, lives, out_type=jnp.float32
    )[0]
    up0, down0, across0, up1, down1, across1, prefix_sent, early0 = phase_end(
        up0, down0, across0, up1, down1, across1, prefix_sent, early0
    )

    far0 = send(up0, 0, 1)
    far1 = send(down1, 0, -1)
    prefix_home = exchange(prefix_sent)
    far0, far1, across0, across1, early0 = phase_end(far0, far1, across0, across1, early0)

    across_up0, across_down0 = send(across0, 0, 1), send(across0, 0, -1)
    across_far0 = send(far0, 1, 0)
    early1 = project(
        [[second], [across1], [up1], [down1], [far1]], ids[:5], both, lives, out_type=jnp.float32
    )[0]
    across_up0, across_down0, across_far0, across1, far1, prefix_home, early1 = phase_end(
        across_up0, across_down0, across_far0, across1, far1, prefix_home, early1
    )

    across_up1, across_down1 = send(across1, 0, 1), send(across1, 0, -1)
    across_far1 = send(far1, 1, 0)
    q0, kv0, spread0 = project(
        [[far0], [across_up0], [across_down0], [across_far0]],
        ids[4:],
        both,
        lives,
        start=early0,
        spread=(per_rep, 0, replicas, True),
    )
    got0 = exchange(spread0)
    out0 = prefill_part(0, 2, q0, prefix_cache, [kv0], fills, lives, None)
    across_up1, across_down1, across_far1, got0, out0, kv0 = phase_end(
        across_up1, across_down1, across_far1, got0, out0, kv0
    )

    late1 = [[across_up1], [across_down1], [across_far1]]
    kv1, spread1 = project(
        late1,
        ids[5:],
        [w_keyval],
        lives,
        start=early1,
        start_col=q_cols,
        spread=(per_rep, half, replicas, False),
    )
    got1 = exchange(spread1)
    q1 = project(late1, ids[5:], [w_query], lives, start=early1)[0]
    dec_back = decode_part(got0, held, prefix_cache, [kv0, kv1], my_owner, fills, lives)
    dec_back, q1 = phase_end(dec_back, q1)
    home = exchange(route([got0, got1], source, block, dec_back))
    earlier = settle(prefix_home, per_rep, ctx_len + new_len)
    decode_cache, decode_out = finish(home, earlier, my_source, block, 2, q_cols)

    prefill_out = prefill_part(1, 2, q1, prefix_cache, [kv0, kv1], fills, lives, out0)
    return (prefill_out, decode_out, decode_cache)


def solution(mesh):
    in_specs = (
        P("replica", "tensor"),
        P("replica", "tensor"),
        P(None, "tensor"),
        P(None, "tensor"),
        P("replica", None, "tensor"),
        P(),
        P(),
        P(),
    )
    out_specs = (P("replica", "tensor"), P("replica", "tensor"), P("replica", None, "tensor"))
    return jax.shard_map(local, mesh=mesh, in_specs=in_specs, out_specs=out_specs, check_vma=False)
```

```python
import functools
import math

import jax
import jax.numpy as jnp
from jax import lax
from jax.experimental import pallas as pl
from jax.experimental.pallas import tpu as pltpu
from jax.sharding import PartitionSpec as P

HEADS = 48
KV = 8
HD = 128
GROUP = HEADS // KV
STEPS = 2
DEC_ROWS = 16
KEY_BLOCK = 256
SMALL_VMEM = 16 * 1024 * 1024
WHOLE_VMEM = 62 * 1024 * 1024

LOW_SCORE = -1e30
EXP_SCALE = math.log2(math.e) / math.sqrt(HD)


def dot_nt(a, b):
    return lax.dot_general(a, b, (((1,), (1,)), ((), ())), preferred_element_type=jnp.float32)


def dot_nn(a, b):
    return lax.dot_general(a, b, (((1,), (0,)), ((), ())), preferred_element_type=jnp.float32)


def row_tiles(counts):
    tiles = []
    start = 0
    for count in counts:
        first = (count // 2 + 15) // 16 * 16
        tiles += [(start, first), (start + first, count - first)]
        start += count
    return tiles


def project_kernel(shape, has_start, start_col, spread, widths, ids, lives, *refs):
    groups, counts, depth = shape
    refs = list(refs)
    pieces = [[refs.pop(0) for _ in counts] for _ in range(groups)]
    weights = [refs.pop(0) for _ in widths]
    start_ref = refs.pop(0) if has_start else None
    held, weight_held, total, sems = refs[-4:]
    outs = refs[:-4]
    offsets = [sum(counts[:i]) for i in range(len(counts))]
    columns = [sum(widths[:i]) for i in range(len(widths))]
    per = 1

    def copies(k):
        made = []
        for j in range(k * per, (k + 1) * per):
            at = pl.ds((j - k * per) * depth, depth)
            for i, count in enumerate(counts):
                made.append((pieces[j][i], held.at[k, pl.ds(offsets[i], count), at]))
            half = depth // 2
            for i, width in enumerate(widths):
                for part in range(2):
                    src = pl.ds(pl.multiple_of(ids[j] * depth + part * half, half), half)
                    dst = pl.ds((j - k * per) * depth + part * half, half)
                    made.append(
                        (
                            weights[i].at[src, :],
                            weight_held.at[k, dst, pl.ds(columns[i], width)],
                        )
                    )
        return [
            pltpu.make_async_copy(src, dst, sems.at[k, n]) for n, (src, dst) in enumerate(made)
        ]

    steps = groups // per
    all_columns = sum(widths)
    for copy in copies(0):
        copy.start()
    if has_start:
        before = pltpu.make_async_copy(
            start_ref.at[:, pl.ds(start_col, all_columns)], total, sems.at[steps, 0]
        )
        before.start()
    for k in range(1, steps):
        for copy in copies(k):
            copy.start()
    for k in range(steps):
        for copy in copies(k):
            copy.wait()
        if k == 0 and has_start:
            before.wait()
        for row, count in row_tiles(counts):
            for col in range(0, all_columns, 512):
                width = min(512, all_columns - col)
                at = (slice(row, row + count), slice(col, col + width))
                part = dot_nn(held[k, row : row + count, :], weight_held[k, :, col : col + width])
                if k or has_start:
                    part = part + total[at]
                if k < steps - 1:
                    total[at] = part
                    continue
                if outs[0].dtype == jnp.float32:
                    group = max(i for i, offset in enumerate(offsets) if offset <= row)
                    low = row - offsets[group]
                    outs[group][low : low + count, col : col + width] = part
                    continue
                for out, first, wide in zip(outs[: len(widths)], columns, widths):
                    low, high = max(first, col), min(first + wide, col + width)
                    if low < high:
                        value = part[:, low - col : high - col].astype(jnp.bfloat16)
                        out[row : row + count, low - first : high - first] = value
    if spread:
        pack(spread, lives, outs)


def pack(spread, lives, outs):
    reqs, first_pos, dests, _ = spread
    q_ref, kv_ref, spread_ref = outs[0], outs[-2], outs[-1]
    columns = kv_ref.shape[1]
    each = kv_ref.shape[0] // reqs // 16 * 16
    block = each // dests
    pos = first_pos + lax.broadcasted_iota(jnp.int32, (each, 1), 0)
    for req in range(reqs):
        rows = kv_ref[req * each : (req + 1) * each, :]
        rows = jnp.where(pos < lives[req], rows, jnp.zeros_like(rows))
        for dest in range(dests):
            spread_ref[dest, req * block : (req + 1) * block, :] = rows[
                dest * block : (dest + 1) * block
            ]
    if spread_ref.shape[1] == reqs * block:
        return
    queries = q_ref[reqs * each :, :].astype(jnp.float32)
    keyvals = kv_ref[reqs * each :, :].astype(jnp.float32)
    slab = []
    for row in range(reqs * STEPS):
        for low in range(0, queries.shape[1], columns):
            slab.append(queries[row : row + 1, low : low + columns])
        slab.append(keyvals[row : row + 1, :])
    slab = jnp.concatenate(slab, axis=0).astype(jnp.bfloat16)
    for dest in range(dests):
        spread_ref[dest, reqs * block :, :] = slab


def project(pieces, ids, weights, lives, start=None, start_col=0, out_type=jnp.bfloat16, spread=None):
    groups = len(pieces)
    counts = tuple(x.shape[0] for x in pieces[0])
    depth = pieces[0][0].shape[1]
    widths = tuple(w.shape[1] for w in weights)
    rows, columns = sum(counts), sum(widths)
    has_start = start is not None
    operands = [x for group in pieces for x in group] + list(weights)
    in_specs = [pl.BlockSpec(memory_space=pltpu.HBM)] * len(operands)
    if has_start:
        in_specs.append(pl.BlockSpec(memory_space=pltpu.HBM))
        operands.append(start)
    if out_type == jnp.float32:
        out_shape = [jax.ShapeDtypeStruct((count, columns), jnp.float32) for count in counts]
    else:
        out_shape = [jax.ShapeDtypeStruct((rows, w), jnp.bfloat16) for w in widths]
    if spread:
        reqs, _, dests, has_dec = spread
        length = rows // reqs // 16 * 16 * reqs // dests
        if has_dec:
            length += reqs * STEPS * (widths[0] // widths[-1] + 1)
        out_shape.append(jax.ShapeDtypeStruct((dests, length, widths[-1]), jnp.bfloat16))
    per = 1
    copies = per * (len(counts) + 2 * len(widths))
    return pl.pallas_call(
        functools.partial(
            project_kernel, (groups, counts, depth), has_start, start_col, spread, widths
        ),
        out_shape=out_shape,
        grid_spec=pltpu.PrefetchScalarGridSpec(
            num_scalar_prefetch=2,
            grid=(1,),
            in_specs=in_specs,
            out_specs=[pl.BlockSpec(memory_space=pltpu.VMEM)] * len(out_shape),
            scratch_shapes=[
                pltpu.VMEM((groups // per, rows, per * depth), jnp.bfloat16),
                pltpu.VMEM((groups // per, per * depth, columns), jnp.bfloat16),
                pltpu.VMEM((rows, columns), jnp.float32),
                pltpu.SemaphoreType.DMA((groups // per + 1, copies)),
            ],
        ),
        compiler_params=pltpu.CompilerParams(
            dimension_semantics=("arbitrary",), vmem_limit_bytes=WHOLE_VMEM
        ),
        cost_estimate=pl.CostEstimate(
            flops=2 * rows * depth * groups * columns,
            bytes_accessed=2 * groups * depth * (rows + columns) + 4 * rows * columns,
            transcendentals=0,
        ),
        name="project",
    )(ids, lives, *operands)


def route_kernel(block, count, source, *refs):
    got_refs, out_ref = refs[:count], refs[-1]
    dests = out_ref.shape[0]
    per_rep = source.shape[0] // dests
    for slot in range(source.shape[0]):
        request = source[slot]
        at = pl.ds(pl.multiple_of((request % per_rep) * block, block), block)
        for part in range(count):
            low = (part * per_rep + slot % per_rep) * block
            out_ref[slot // per_rep, low : low + block, :] = got_refs[part][
                request // per_rep, at, :
            ]
    low = count * per_rep * block
    for extra_ref in refs[count:-1]:
        for dest in range(dests):
            out_ref[dest, low : low + extra_ref.shape[0], :] = extra_ref[...]


def route(got, source, block, *extra):
    dests, _, columns = got[0].shape
    per_rep = source.shape[0] // dests
    length = len(got) * per_rep * block + sum(x.shape[0] for x in extra)
    operands = [*got, *extra]
    return pl.pallas_call(
        functools.partial(route_kernel, block, len(got)),
        out_shape=jax.ShapeDtypeStruct((dests, length, columns), got[0].dtype),
        grid_spec=pltpu.PrefetchScalarGridSpec(
            num_scalar_prefetch=1,
            grid=(1,),
            in_specs=[pl.BlockSpec(memory_space=pltpu.VMEM)] * len(operands),
            out_specs=pl.BlockSpec(memory_space=pltpu.VMEM),
        ),
        compiler_params=pltpu.CompilerParams(vmem_limit_bytes=SMALL_VMEM),
        cost_estimate=pl.CostEstimate(
            flops=0, bytes_accessed=4 * dests * length * columns, transcendentals=0
        ),
        name="route",
    )(source, *operands)


def settle_kernel(got_ref, out_ref):
    dests, length, _ = got_ref.shape
    block = out_ref.shape[1] // dests
    at = pl.ds(pl.multiple_of(pl.program_id(0) * block, block), block)
    for dest in range(dests):
        out_ref[0, dest * block : (dest + 1) * block, :] = got_ref[dest, at, :]


def settle(got, per_rep, total_len):
    dests, length, columns = got.shape
    held = dests * length // per_rep
    return pl.pallas_call(
        settle_kernel,
        out_shape=jax.ShapeDtypeStruct((per_rep, total_len, columns), got.dtype),
        grid=(per_rep,),
        in_specs=[pl.BlockSpec(memory_space=pltpu.VMEM)],
        out_specs=pl.BlockSpec((1, held, columns), lambda c: (c, 0, 0)),
        compiler_params=pltpu.CompilerParams(vmem_limit_bytes=SMALL_VMEM),
        name="settle",
    )(got)


def finish_kernel(block, count, source, home_ref, earlier_ref, cache_ref, out_ref):
    dests, _, columns = home_ref.shape
    per_rep = out_ref.shape[0] // STEPS
    slot = pl.program_id(0)
    for part in range(count):
        at = pl.ds(pl.multiple_of((part * per_rep + slot) * block, block), block)
        for dest in range(dests):
            low = (part * dests + dest) * block
            cache_ref[0, low : low + block, :] = home_ref[dest, at, :]

    @pl.when(slot == 0)
    def _():
        low = count * per_rep * block
        for mine in range(per_rep):
            request = source[mine]
            both = home_ref[request // per_rep, low : low + 16, :].astype(jnp.float32)
            rows = jnp.where(request % per_rep == 0, both[:8], both[8:])
            for step in range(STEPS):
                for part in range(out_ref.shape[1] // columns):
                    row = step * (8 // STEPS) + part
                    at = mine * STEPS + step
                    out_ref[at : at + 1, part * columns : (part + 1) * columns] = rows[
                        row : row + 1
                    ].astype(jnp.bfloat16)


def finish(home, earlier, source, block, count, q_cols):
    dests, _, columns = home.shape
    per_rep, total_len, _ = earlier.shape
    new_len = count * dests * block
    return pl.pallas_call(
        functools.partial(finish_kernel, block, count),
        out_shape=(
            jax.ShapeDtypeStruct(earlier.shape, earlier.dtype),
            jax.ShapeDtypeStruct((per_rep * STEPS, q_cols), earlier.dtype),
        ),
        grid_spec=pltpu.PrefetchScalarGridSpec(
            num_scalar_prefetch=1,
            grid=(per_rep,),
            in_specs=[
                pl.BlockSpec(memory_space=pltpu.VMEM),
                pl.BlockSpec(memory_space=pltpu.HBM),
            ],
            out_specs=(
                pl.BlockSpec((1, new_len, columns), lambda c, *_: (c, total_len // new_len - 1, 0)),
                pl.BlockSpec(memory_space=pltpu.VMEM),
            ),
        ),
        input_output_aliases={2: 0},
        compiler_params=pltpu.CompilerParams(vmem_limit_bytes=SMALL_VMEM),
        name="finish",
    )(source, home, earlier)


def phase_end(*arrays):
    return lax.optimization_barrier(arrays)


def prefill_kernel(parts, ctx_len, fill_ref, live_ref, q_ref, prefix_ref, *refs):
    kv_refs = refs[: parts + 1]
    out_ref = refs[-1]
    req = pl.program_id(0)
    fill = fill_ref[req]
    live = live_ref[req]
    rows = q_ref.shape[0]
    first_row = parts * rows
    row_ids = lax.broadcasted_iota(jnp.int32, (rows, 1), 0)
    own_ids = lax.broadcasted_iota(jnp.int32, (rows, rows), 1)
    causal = own_ids <= lax.broadcasted_iota(jnp.int32, (rows, rows), 0)

    def heads(blocks):
        seen = blocks * KEY_BLOCK
        last = seen - KEY_BLOCK
        last_live = last + lax.broadcasted_iota(jnp.int32, (rows, KEY_BLOCK), 1) < fill

        def one_head(h):
            cols = pl.ds(pl.multiple_of(h * HD, HD), HD)
            query = q_ref[:, cols]
            scores = []
            if last:
                scores.append(dot_nt(query, prefix_ref[0, :last, :HD]))
            scores.append(
                jnp.where(last_live, dot_nt(query, prefix_ref[0, last:seen, :HD]), LOW_SCORE)
            )
            for part in range(parts):
                scores.append(dot_nt(query, kv_refs[part][:, :HD]))
            scores.append(jnp.where(causal, dot_nt(query, kv_refs[parts][:, :HD]), LOW_SCORE))
            top = scores[0].max(axis=1, keepdims=True)
            for score in scores[1:]:
                top = jnp.maximum(top, score.max(axis=1, keepdims=True))
            weights = [jnp.exp2((score - top) * EXP_SCALE) for score in scores]
            total = weights[0].sum(axis=1, keepdims=True)
            for weight in weights[1:]:
                total = total + weight.sum(axis=1, keepdims=True)
            weights = [weight.astype(jnp.bfloat16) for weight in weights]
            mixed = None
            values = []
            if last:
                values.append(prefix_ref[0, :last, HD:])
            values.append(prefix_ref[0, last:seen, HD:])
            for part in range(parts + 1):
                values.append(kv_refs[part][:, HD:])
            for weight, value in zip(weights, values):
                term = dot_nn(weight, value)
                mixed = term if mixed is None else mixed + term
            mixed = mixed / total
            if parts:
                mixed = jnp.where(first_row + row_ids < live, mixed, 0.0)
            out_ref[:, cols] = mixed.astype(jnp.bfloat16)

        @pl.loop(0, GROUP // 3)
        def _(triple):
            for n in range(3):
                one_head(3 * triple + n)

    block_count = (fill + KEY_BLOCK - 1) // KEY_BLOCK
    is_live = first_row < live
    for blocks in range(1, ctx_len // KEY_BLOCK + 1):

        @pl.when((block_count == blocks) & is_live)
        def _(blocks=blocks):
            heads(blocks)

    @pl.when(jnp.logical_not(is_live))
    def _():
        out_ref[...] = jnp.zeros_like(out_ref)


def prefill_part(part, part_count, queries, prefix, keyvals, fills, lives, earlier_out):
    cols = queries.shape[1]
    reqs, ctx_len, pair_cols = prefix.shape
    rows = queries.shape[0] // reqs // 16 * 16
    in_specs = [
        pl.BlockSpec((rows, cols), lambda r, *_: (r, 0)),
        pl.BlockSpec((1, ctx_len, pair_cols), lambda r, *_: (r, 0, 0)),
    ]
    in_specs += [pl.BlockSpec((rows, pair_cols), lambda r, *_: (r, 0))] * (part + 1)
    operands = [queries, prefix, *keyvals[: part + 1]]
    aliases = {}
    if earlier_out is not None:
        in_specs.append(pl.BlockSpec(memory_space=pl.ANY))
        aliases = {2 + len(operands): 0}
        operands.append(earlier_out)
    return pl.pallas_call(
        functools.partial(prefill_kernel, part, ctx_len),
        out_shape=jax.ShapeDtypeStruct((reqs * part_count * rows, cols), jnp.bfloat16),
        grid_spec=pltpu.PrefetchScalarGridSpec(
            num_scalar_prefetch=2,
            grid=(reqs,),
            in_specs=in_specs,
            out_specs=pl.BlockSpec((rows, cols), lambda r, *_: (r * part_count + part, 0)),
        ),
        input_output_aliases=aliases,
        compiler_params=pltpu.CompilerParams(
            dimension_semantics=("arbitrary",), vmem_limit_bytes=WHOLE_VMEM
        ),
        cost_estimate=pl.CostEstimate(
            flops=4 * reqs * rows * cols * (ctx_len + rows),
            bytes_accessed=2 * reqs * (2 * rows * cols + ctx_len * pair_cols),
            transcendentals=reqs * rows * (cols // HD) * (ctx_len + rows),
        ),
        name="prefill",
    )(fills, lives, *operands)


def decode_kernel(parts, held, owner_ref, fill_ref, live_ref, got_ref, prefix_ref, *refs):
    kv_refs = refs[:parts]
    out_ref = refs[-1]
    reqs = prefix_ref.shape[0]
    ctx_len = prefix_ref.shape[1]
    part_len = kv_refs[0].shape[0] // reqs // 16 * 16
    half = out_ref.shape[0] // reqs

    def live_where(count, limit, scores):
        return jnp.where(
            lax.broadcasted_iota(jnp.int32, scores.shape, 1) < limit, scores, LOW_SCORE
        )

    for req in range(reqs):
        slot = owner_ref[req]
        fill = fill_ref[req]
        live = live_ref[req]
        both = got_ref[slot // reqs, held : held + 2 * half, :].astype(jnp.float32)
        slab = jnp.where(slot % reqs == 0, both[:half], both[half:])
        query = jnp.concatenate([slab[:, :HD], slab[:, HD:]], axis=0).astype(jnp.bfloat16)
        rows = query.shape[0]
        scores = [live_where(ctx_len, fill, dot_nt(query, prefix_ref[req, :, :HD]))]
        values = [prefix_ref[req, :, HD:]]
        for part in range(parts):
            part_scores = dot_nt(query, kv_refs[part][req * part_len : (req + 1) * part_len, :HD])
            scores.append(live_where(part_len, live - part * part_len, part_scores))
            values.append(kv_refs[part][req * part_len : (req + 1) * part_len, HD:])
        own_scores = dot_nt(query, query)
        row_ids = lax.broadcasted_iota(jnp.int32, own_scores.shape, 0)
        key_ids = lax.broadcasted_iota(jnp.int32, own_scores.shape, 1)
        per_step = half // STEPS
        is_key = (key_ids < half) & (key_ids % per_step == per_step - 1)
        seen = key_ids // per_step <= row_ids % half // per_step
        scores.append(jnp.where(is_key & seen, own_scores, LOW_SCORE))
        own_values = slab[:, HD:].astype(jnp.bfloat16)
        values.append(jnp.concatenate([own_values, own_values], axis=0))
        top = scores[0].max(axis=1, keepdims=True)
        for score in scores[1:]:
            top = jnp.maximum(top, score.max(axis=1, keepdims=True))
        total = jnp.zeros((rows, 1), jnp.float32)
        mixed = jnp.zeros((rows, HD), jnp.float32)
        for score, value in zip(scores, values):
            weight = jnp.exp2((score - top) * EXP_SCALE)
            total = total + weight.sum(axis=1, keepdims=True)
            coarse = weight.astype(jnp.bfloat16)
            fine = (weight - coarse.astype(jnp.float32)).astype(jnp.bfloat16)
            mixed = mixed + dot_nn(coarse, value) + dot_nn(fine, value)
        mixed = mixed / total
        out_ref[req * half : (req + 1) * half, :HD] = mixed[:half].astype(jnp.bfloat16)
        out_ref[req * half : (req + 1) * half, HD:] = mixed[half:].astype(jnp.bfloat16)


def decode_part(got, held, prefix, keyvals, owners, fills, lives):
    reqs = prefix.shape[0]
    blocks = [got, prefix, *keyvals]
    slab = reqs * STEPS * (GROUP // 2 + 1)
    return pl.pallas_call(
        functools.partial(decode_kernel, len(keyvals), held),
        out_shape=jax.ShapeDtypeStruct((slab, got.shape[2]), jnp.bfloat16),
        grid_spec=pltpu.PrefetchScalarGridSpec(
            num_scalar_prefetch=3,
            grid=(1,),
            in_specs=[pl.BlockSpec(memory_space=pltpu.VMEM) for _ in blocks],
            out_specs=pl.BlockSpec(memory_space=pltpu.VMEM),
        ),
        compiler_params=pltpu.CompilerParams(
            dimension_semantics=("arbitrary",), vmem_limit_bytes=WHOLE_VMEM
        ),
        cost_estimate=pl.CostEstimate(
            flops=6 * slab * HD * 1536,
            bytes_accessed=2 * reqs * 1536 * 2 * HD,
            transcendentals=slab * 1536,
        ),
        name="decode",
    )(owners, fills, lives, *blocks)


def local(prompt, dec_tokens, w_query, w_keyval, prefix_cache, prompt_len, fill_len, owner):
    replicas = lax.axis_size("replica")
    tensors = lax.axis_size("tensor")
    ring = tensors // 2
    replica_id = lax.axis_index("replica")
    tensor_id = lax.axis_index("tensor")
    per_rep, ctx_len, pair_cols = prefix_cache.shape
    new_len = prompt.shape[0] // per_rep
    depth = prompt.shape[1]
    q_cols = w_query.shape[1]
    half = new_len // 2
    request_count = per_rep * replicas
    first_req = replica_id * per_rep

    def moved(plane, shift):
        return [
            (p * ring + y, ((p + plane) % 2) * ring + (y + shift) % ring)
            for p in range(2)
            for y in range(ring)
        ]

    def send(x, plane, shift):
        return lax.ppermute(x, "tensor", moved(plane, shift))

    my_plane, my_y = tensor_id // ring, tensor_id % ring

    def block_id(plane, shift):
        return ((my_plane + plane) % 2) * ring + (my_y + shift + ring) % ring

    ids = jnp.stack(
        [
            block_id(0, 0),
            block_id(1, 0),
            block_id(0, -1),
            block_id(0, 1),
            block_id(0, 2),
            block_id(1, -1),
            block_id(1, 1),
            block_id(1, 2),
        ]
    ).astype(jnp.int32)

    slot_ids = jnp.arange(request_count, dtype=jnp.int32)
    source = jnp.sum(jnp.where(owner[None, :] == slot_ids[:, None], slot_ids[None, :], 0), axis=1)
    fills = lax.dynamic_slice_in_dim(fill_len, first_req, per_rep, 0)
    lives = lax.dynamic_slice_in_dim(prompt_len, first_req, per_rep, 0)
    my_owner = lax.dynamic_slice_in_dim(owner, first_req, per_rep, 0)
    my_source = lax.dynamic_slice_in_dim(source, first_req, per_rep, 0)

    def exchange(x):
        return lax.all_to_all(x, "replica", split_axis=0, concat_axis=0, tiled=True)

    def zero_dead(x, first_pos, counts):
        pos = first_pos + jnp.arange(x.shape[1], dtype=jnp.int32)
        return jnp.where((pos[None, :] < counts[:, None])[:, :, None], x, jnp.zeros((), x.dtype))

    def for_spread(x):
        block = x.shape[1] // replicas
        return x.reshape(per_rep, replicas, block, pair_cols).transpose(1, 0, 2, 3).reshape(
            replicas, per_rep * block, pair_cols
        )

    rows = per_rep * half
    both = [w_query, w_keyval]
    block = half // replicas
    held = per_rep * block
    dec_pad = jnp.pad(dec_tokens, ((0, DEC_ROWS - dec_tokens.shape[0]), (0, 0)))
    by_req = prompt.reshape(per_rep, 2, half, depth)
    first = jnp.concatenate([by_req[:, 0].reshape(rows, depth), dec_pad], axis=0)
    second = by_req[:, 1].reshape(rows, depth)

    up0, down0, across0 = send(first, 0, 1), send(first, 0, -1), send(first, 1, 0)
    up1, down1 = send(second, 0, 1), send(second, 0, -1)
    prefix_got = exchange(for_spread(zero_dead(prefix_cache, 0, fills)))
    prefix_sent = route([prefix_got], source, ctx_len // replicas)
    early0 = project(
        [[first], [across0], [up0], [down0]], ids[:4], both, lives, out_type=jnp.float32
    )[0]
    up0, down0, across0, up1, down1, second, prefix_sent, early0 = phase_end(
        up0, down0, across0, up1, down1, second, prefix_sent, early0
    )

    far0 = send(up0, 0, 1)
    far1 = send(down1, 0, -1)
    across1 = send(second, 1, 0)
    prefix_home = exchange(prefix_sent)
    far0, far1, across0, early0 = phase_end(far0, far1, across0, early0)

    across_up0, across_down0 = send(across0, 0, 1), send(across0, 0, -1)
    across_far0 = send(far0, 1, 0)
    early1 = project(
        [[second], [across1], [up1], [down1], [far1]], ids[:5], both, lives, out_type=jnp.float32
    )[0]
    across_up0, across_down0, across_far0, across1, far1, prefix_home, early1 = phase_end(
        across_up0, across_down0, across_far0, across1, far1, prefix_home, early1
    )

    across_up1, across_down1 = send(across1, 0, 1), send(across1, 0, -1)
    across_far1 = send(far1, 1, 0)
    q0, kv0, spread0 = project(
        [[far0], [across_up0], [across_down0], [across_far0]],
        ids[4:],
        both,
        lives,
        start=early0,
        spread=(per_rep, 0, replicas, True),
    )
    got0 = exchange(spread0)
    out0 = prefill_part(0, 2, q0, prefix_cache, [kv0], fills, lives, None)
    across_up1, across_down1, across_far1, got0, out0, kv0 = phase_end(
        across_up1, across_down1, across_far1, got0, out0, kv0
    )

    late1 = [[across_up1], [across_down1], [across_far1]]
    kv1, spread1 = project(
        late1,
        ids[5:],
        [w_keyval],
        lives,
        start=early1,
        start_col=q_cols,
        spread=(per_rep, half, replicas, False),
    )
    got1 = exchange(spread1)
    q1 = project(late1, ids[5:], [w_query], lives, start=early1)[0]
    dec_back = decode_part(got0, held, prefix_cache, [kv0, kv1], my_owner, fills, lives)
    dec_back, q1 = phase_end(dec_back, q1)
    home = exchange(route([got0, got1], source, block, dec_back))
    earlier = settle(prefix_home, per_rep, ctx_len + new_len)
    decode_cache, decode_out = finish(home, earlier, my_source, block, 2, q_cols)

    prefill_out = prefill_part(1, 2, q1, prefix_cache, [kv0, kv1], fills, lives, out0)
    return (prefill_out, decode_out, decode_cache)


def solution(mesh):
    in_specs = (
        P("replica", "tensor"),
        P("replica", "tensor"),
        P(None, "tensor"),
        P(None, "tensor"),
        P("replica", None, "tensor"),
        P(),
        P(),
        P(),
    )
    out_specs = (P("replica", "tensor"), P("replica", "tensor"), P("replica", None, "tensor"))
    return jax.shard_map(local, mesh=mesh, in_specs=in_specs, out_specs=out_specs, check_vma=False)
```
